32 devices in a mesh: scan: 16 (over z, y, x), mode: 2 (over core).
Axes of the slice: x: 2, y: 2, z: 4, core: 2. Of those that a mesh axis runs over, the one named last changes fastest.
Arguments:
- object_field: float32 [2, 640, 1152], P(None, 'scan'), may hold values from -4.5 to 4.5
- probe: float32 [8, 2, 512, 512], P('mode'), may hold values from -1.5 to 1.5
- amplitude: float32 [16, 512, 512], P('scan'), may hold values from 0.2 to 1.8
- pos_row: int32 [16], P('scan'), may hold values from 0 to 128, as said below
- pos_col: int32 [16], P('scan'), may hold values from 0 to 640, as said below
- strip_of: int32 [16], P('scan'), may hold values from 0 to 15, each once
Outputs:
- object_grad: float32 [2, 640, 1152], P(None, 'scan')
- probe_grad: float32 [8, 2, 512, 512], P('mode')
The draws below stay inside these ranges and needn't reach their ends.
Inputs may be any that keep to these rules, and one draw needn't show every extreme that they name: Pattern p covers object rows pos_row[p] to pos_row[p] + 511; the smallest and the largest allowed value both occur. Pattern p covers object columns pos_col[p] to pos_col[p] + 511; the smallest and the largest allowed value both occur.
All inputs are finite; a program needn't handle non-finite values.
Results may differ from the reference program's by a relative error of at most 0.0055.
The reference program's roundings to bfloat16 on the way count: a program that leaves them out, or rounds other values in their place, can miss the bound.
Values may be sent and summed in bfloat16 or wider, within the bound.
A program may use at most 128 MiB of HBM per device.

```python
import math
import jax
import jax.numpy as jnp
from jax import lax

PROBE = 512
MODES = 8
COLS = 1152
STRIP = 40
PATTERNS = 16
TILES = 16
OBJ_ROWS = 640


def pinned_offsets(key, count_all, upper_bound):
    first_key, second_key, third_key = jax.random.split(key, 3)
    values = jax.random.randint(first_key, (count_all,), 0, upper_bound + 1, dtype=jnp.int32)
    low_slot = jax.random.randint(second_key, (), 0, count_all, dtype=jnp.int32)
    shift_by = jax.random.randint(third_key, (), 1, count_all, dtype=jnp.int32)
    high_slot = (low_slot + shift_by) % count_all
    slots = jnp.arange(count_all, dtype=jnp.int32)
    values = jnp.where(slots == low_slot, 0, values)
    return jnp.where(slots == high_slot, upper_bound, values).astype(jnp.int32)


def draw_pos_row(key, part):
    return pinned_offsets(jax.random.fold_in(key, 11), PATTERNS, OBJ_ROWS - PROBE)


def draw_pos_col(key, part):
    return pinned_offsets(jax.random.fold_in(key, 23), PATTERNS, COLS - PROBE)


def shard_levels(key, shape, cuts, low, largest):
    level = 1.0
    for position, shards_of in cuts:
        draws = jax.random.uniform(jax.random.fold_in(jax.random.fold_in(key, 6), position), (shards_of,), jnp.float32, low / len(cuts), largest / len(cuts))
        level = level * jnp.repeat(jnp.exp(draws), shape[position] // shards_of).reshape((-1,) + (1,) * (len(shape) - 1 - position))
    return level


def centred(own_key, extent, spread, reach, cuts=(), kind=jnp.bfloat16):
    loudness = shard_levels(own_key, extent, cuts, -0.22, 0.18) if cuts else 1.0
    values = jax.random.normal(own_key, extent, jnp.float32) * spread * loudness
    return jnp.minimum(jnp.maximum(values, -reach), reach).astype(kind)


def setup_inputs(seed: int = 0) -> dict:
    keys = jax.random.split(jax.random.key(seed), 7)
    object_field = centred(keys[0], (2, OBJ_ROWS, COLS), 0.7, 4.5, ((1, 16),), jnp.float32)
    probe = centred(keys[1], (MODES, 2, PROBE, PROBE), 0.25, 1.5, ((0, 2),), jnp.float32)
    amplitude = jnp.clip(0.2 + 1.5999999 * jax.random.uniform(keys[2], (PATTERNS, PROBE, PROBE), jnp.float32) ** shard_levels(keys[2], (PATTERNS, PROBE, PROBE), ((0, 16),), -0.2, 0.2), 0.2, 1.8)
    pos_row = draw_pos_row(jax.random.fold_in(keys[6], 71), 0)
    pos_col = draw_pos_col(jax.random.fold_in(keys[6], 71), 0)
    strip_of = jax.random.permutation(keys[5], TILES).astype(jnp.int32)
    return {"object_field": object_field, "probe": probe, "amplitude": amplitude, "pos_row": pos_row, "pos_col": pos_col, "strip_of": strip_of}


def dft_table(sign_factor):
    positions = jnp.arange(PROBE, dtype=jnp.int32)
    products = positions[:, None] * positions[None, :] % PROBE
    angle_table = products.astype(jnp.float32) * (2.0 * math.pi / PROBE)
    norm_scale = 1.0 / math.sqrt(PROBE)
    cosine = jnp.cos(angle_table) * norm_scale
    sine_part = jnp.sin(angle_table) * (sign_factor * norm_scale)
    table_half = jnp.stack([jnp.stack([cosine, sine_part]), jnp.stack([-sine_part, cosine])]).astype(jnp.bfloat16)
    return lax.optimization_barrier(table_half)

def transform(field_wave, matrix_table):
    table_wide = matrix_table.astype(jnp.float32)
    half_wave = jnp.einsum('oiab,mibx->moax', table_wide, field_wave.astype(jnp.float32))
    half_wave = lax.optimization_barrier(half_wave.astype(jnp.bfloat16))
    return jnp.einsum('miax,oixy->moay', half_wave.astype(jnp.float32), table_wide)

def reference(object_field, probe, amplitude, pos_row, pos_col, strip_of):
    forward = dft_table(1.0)
    inverse = dft_table(-1.0)
    held_strips = object_field.reshape(2, TILES, STRIP, COLS)
    window_field = jnp.zeros_like(held_strips).at[:, strip_of].set(held_strips).reshape(2, OBJ_ROWS, COLS)
    probe_re = probe[:, 0]
    probe_im = probe[:, 1]
    zero_index = jnp.zeros((), jnp.int32)

    def one_pattern(carry, inputs):
        window_grad, probe_grad = carry
        row_start, col_start, measured = inputs
        start = (zero_index, row_start.astype(jnp.int32), col_start.astype(jnp.int32))
        patch_half = lax.optimization_barrier(lax.dynamic_slice(window_field, start, (2, PROBE, PROBE)).astype(jnp.bfloat16))
        patch_wide = patch_half.astype(jnp.float32)
        patch_re = patch_wide[0]
        patch_im = patch_wide[1]
        exit_re = probe_re * patch_re - probe_im * patch_im
        exit_im = probe_re * patch_im + probe_im * patch_re
        exit_wave = lax.optimization_barrier(jnp.stack([exit_re, exit_im], axis=1).astype(jnp.bfloat16))
        far_field = transform(exit_wave, forward)
        intensity = lax.optimization_barrier(jnp.sum(far_field[:, 0] * far_field[:, 0] + far_field[:, 1] * far_field[:, 1], axis=0))
        scale_factor = 1.0 - measured / jnp.sqrt(jnp.maximum(intensity, 0.25))
        residual_wave = lax.optimization_barrier((far_field * scale_factor).astype(jnp.bfloat16))
        back_wave = transform(residual_wave, inverse)
        back_re = back_wave[:, 0]
        back_im = back_wave[:, 1]
        grad_re = lax.optimization_barrier(jnp.sum(probe_re * back_re + probe_im * back_im, axis=0))
        grad_im = lax.optimization_barrier(jnp.sum(probe_re * back_im - probe_im * back_re, axis=0))
        current = lax.dynamic_slice(window_grad, start, (2, PROBE, PROBE))
        window_grad = lax.dynamic_update_slice(window_grad, current + jnp.stack([grad_re, grad_im]), start)
        term_re = patch_re * back_re + patch_im * back_im
        term_im = patch_re * back_im - patch_im * back_re
        probe_grad = probe_grad + jnp.stack([term_re, term_im], axis=1)
        return ((window_grad, probe_grad), None)
    initial = (jnp.zeros((2, OBJ_ROWS, COLS), jnp.float32), jnp.zeros((MODES, 2, PROBE, PROBE), jnp.float32))
    (window_grad, probe_grad), _ = lax.scan(one_pattern, initial, (pos_row, pos_col, amplitude))
    object_grad = window_grad.reshape(2, TILES, STRIP, COLS)[:, strip_of].reshape(2, OBJ_ROWS, COLS)
    return (object_grad, probe_grad)
```

```python
import math

import jax
import jax.numpy as jnp
import numpy as np
from jax import lax
from jax.experimental import pallas as pl
from jax.experimental.pallas import tpu as pltpu
from jax.sharding import PartitionSpec as P

F32 = jnp.float32
BF16 = jnp.bfloat16
LANES = 128
META = 16
TILE = 256
PARAMS = pltpu.CompilerParams(vmem_limit_bytes=56 * 1024 * 1024)
VMEM = pl.BlockSpec(memory_space=pltpu.VMEM)
SMEM = pl.BlockSpec(memory_space=pltpu.SMEM)


def dft_tables(size):
    positions = np.arange(size, dtype=np.int32)
    angles = (positions[:, None] * positions[None, :] % size).astype(np.float32)
    angles = angles * np.float32(2.0 * math.pi / size)
    norm = np.float32(1.0 / math.sqrt(size))
    cosine, sine = np.cos(angles) * norm, np.sin(angles) * norm
    forward = np.block([[cosine, sine], [-sine, cosine]])
    inverse = np.block([[cosine, -sine], [sine, cosine]])
    return jnp.asarray(forward, BF16), jnp.asarray(inverse, BF16)


def cut_kernel(strips, row, col, held, patch, window):
    count, rows = held.shape[0], (held.shape[1] - META) // 2
    size, cols = patch.shape[-1], held.shape[-1]
    wide = size + LANES

    def place(j, carry):
        both = held[j][: 2 * rows].astype(F32)
        at = pl.ds(pl.multiple_of(strips[j] * rows, 8), rows)
        window[0, at, :cols] = both[:rows]
        window[1, at, :cols] = both[rows:]
        return carry

    lax.fori_loop(0, count, place, 0)
    across = pl.ds(pl.multiple_of(col[0] // LANES * LANES, LANES), wide)
    back = lax.rem(wide - lax.rem(col[0], LANES), wide)
    up = lax.rem(72 - lax.rem(row[0], 8), 72)
    for c in range(2):

        def cut(i, carry, c=c):
            block = window[c, pl.ds(pl.multiple_of(row[0] // 8 * 8 + i * 64, 8), 72), across]
            block = pltpu.roll(block, up, 0)[:64]
            patch[c, pl.ds(pl.multiple_of(i * 64, 64), 64), :] = pltpu.roll(block, back, 1)[:, :size]
            return carry

        lax.fori_loop(0, size // 64, cut, 0)


def forward_kernel(probe, patch, left, right, far, power, wave, half):
    size = patch.shape[-1]

    def leave(i, carry):
        at = pl.ds(pl.multiple_of(i * 64, 64), 64)
        low = pl.ds(pl.multiple_of(size + i * 64, 64), 64)
        pr, pi, xr, xi = probe[0, 0, at], probe[0, 1, at], patch[0, at], patch[1, at]
        wave[at] = (pr * xr - pi * xi).astype(BF16)
        wave[low] = (pr * xi + pi * xr).astype(BF16)
        return carry

    lax.fori_loop(0, size // 64, leave, 0)
    rows_product(left, wave, half)
    first = pl.program_id(0) == 0

    def across(i, carry):
        at = pl.ds(pl.multiple_of(i * TILE, TILE), TILE)
        both = jnp.dot(half[at], right[...], preferred_element_type=F32)
        re, im = both[:, :size], both[:, size:]
        far[0, 0, at] = re
        far[0, 1, at] = im
        here = re * re + im * im
        power[at] = jnp.where(first, here, power[at] + here)
        return carry

    lax.fori_loop(0, size // TILE, across, 0)


def rows_product(left, wave, half):
    size = wave.shape[-1]
    for c in range(2):

        def down(i, carry, c=c):
            at = pl.ds(pl.multiple_of(c * size + i * TILE, TILE), TILE)
            to = pl.ds(pl.multiple_of(i * TILE, TILE), TILE)
            product = jnp.dot(left[at], wave[...], preferred_element_type=F32)
            half[to, c * size : (c + 1) * size] = product.astype(BF16)
            return carry

        lax.fori_loop(0, size // TILE, down, 0)


def backward_kernel(far, probe, patch, measured, power, left, right, term, grad, scale, wave, half):
    size = patch.shape[-1]
    first = pl.program_id(0) == 0

    @pl.when(first)
    def _():
        total = jnp.maximum(power[...], 0.25)
        scale[...] = 1.0 - measured[...] / jnp.sqrt(total)

    def residual(i, carry):
        at = pl.ds(pl.multiple_of(i * 64, 64), 64)
        low = pl.ds(pl.multiple_of(size + i * 64, 64), 64)
        wave[at] = (far[0, 0, at] * scale[at]).astype(BF16)
        wave[low] = (far[0, 1, at] * scale[at]).astype(BF16)
        return carry

    lax.fori_loop(0, size // 64, residual, 0)
    rows_product(left, wave, half)

    def across(i, carry):
        at = pl.ds(pl.multiple_of(i * TILE, TILE), TILE)
        both = jnp.dot(half[at], right[...], preferred_element_type=F32)
        br, bi = both[:, :size], both[:, size:]
        pr, pi, xr, xi = probe[0, 0, at], probe[0, 1, at], patch[0, at], patch[1, at]
        term[0, 0, at] = (xr * br + xi * bi).astype(BF16)
        term[0, 1, at] = (xr * bi - xi * br).astype(BF16)
        re, im = pr * br + pi * bi, pr * bi - pi * br
        grad[0, at] = jnp.where(first, re, grad[0, at] + re)
        grad[1, at] = jnp.where(first, im, grad[1, at] + im)
        return carry

    lax.fori_loop(0, size // TILE, across, 0)


def place_kernel(strips, row, grad, out, padded):
    count, parts, rows, size = out.shape
    padded[...] = jnp.zeros_like(padded)
    padded[:, rows : rows + size, :] = grad[...]

    def one(j, carry):
        start = jnp.clip(strips[j] * rows - row[0], -rows, size) + rows
        base = pl.ds(pl.multiple_of(start // 8 * 8, 8), rows + 8)
        up = lax.rem(rows + 8 - lax.rem(start, 8), rows + 8)
        for k in range(parts):
            out[j, k] = pltpu.roll(padded[k, base, :], up, 0)[:rows]
        return carry

    lax.fori_loop(0, count, one, 0)


def add_kernel(cols, received, out, total):
    count, parts, rows, size = received.shape
    total[...] = jnp.zeros_like(total)
    edge = jnp.zeros((rows, LANES), F32)

    def one(j, carry):
        across = pl.ds(pl.multiple_of(cols[j] // LANES * LANES, LANES), size + LANES)
        shift = lax.rem(cols[j], LANES)
        for k in range(parts):
            piece = jnp.concatenate([received[j, k], edge], axis=1)
            total[k, :, across] += pltpu.roll(piece, shift, 1)
        return carry

    lax.fori_loop(0, count, one, 0)
    out[...] = total[:, :, : out.shape[-1]]


def shards(object_field, probe, amplitude, pos_row, pos_col, strip_of):
    size = probe.shape[-1]
    modes = probe.shape[0]
    rows, cols = object_field.shape[1], object_field.shape[2]
    devices, groups = lax.axis_size("scan"), lax.axis_size("mode")
    padded_cols = cols + LANES
    forward, inverse = dft_tables(size)

    def swap(x):
        return lax.ppermute(x, "mode", [(0, 1), (1, 0)])

    lane = lax.broadcasted_iota(jnp.int32, (META, cols), 1)
    numbers = jnp.where(lane == 0, strip_of[0], jnp.where(lane == 1, pos_col[0] // LANES, pos_col[0] % LANES))
    packed = jnp.concatenate([object_field.reshape(2 * rows, cols).astype(BF16), numbers.astype(BF16)])
    held = lax.all_gather(packed, "scan", axis=0)
    numbers = held[:, 2 * rows, :3].astype(jnp.int32)
    strips = numbers[:, 0]
    all_cols = numbers[:, 1] * LANES + numbers[:, 2]

    wave_shape = jax.ShapeDtypeStruct((2, size, size), F32)
    patch = pl.pallas_call(
        cut_kernel,
        out_shape=wave_shape,
        in_specs=[SMEM, SMEM, SMEM, VMEM],
        out_specs=VMEM,
        scratch_shapes=[pltpu.VMEM((2, devices * rows + 8, padded_cols), F32)],
        compiler_params=PARAMS,
    )(strips, pos_row, pos_col, held)

    def whole(*shape):
        return pl.BlockSpec(shape, lambda m: (0,) * len(shape))

    mode_spec = pl.BlockSpec((1, 2, size, size), lambda m: (m, 0, 0, 0))
    table_spec = whole(2 * size, 2 * size)
    buffers = [pltpu.VMEM((2 * size, size), BF16), pltpu.VMEM((size, 2 * size), BF16)]
    far, power = pl.pallas_call(
        forward_kernel,
        grid=(modes,),
        out_shape=(
            jax.ShapeDtypeStruct((modes, 2, size, size), F32),
            jax.ShapeDtypeStruct((size, size), F32),
        ),
        in_specs=[mode_spec, whole(2, size, size), table_spec, table_spec],
        out_specs=(mode_spec, whole(size, size)),
        scratch_shapes=buffers,
        compiler_params=PARAMS,
    )(probe, patch, forward, inverse)
    power = power + swap(power) if groups == 2 else lax.psum(power, "mode")
    term, grad = pl.pallas_call(
        backward_kernel,
        grid=(modes,),
        out_shape=(jax.ShapeDtypeStruct((modes, 2, size, size), BF16), wave_shape),
        in_specs=[
            mode_spec,
            mode_spec,
            whole(2, size, size),
            whole(size, size),
            whole(size, size),
            table_spec,
            table_spec,
        ],
        out_specs=(mode_spec, whole(2, size, size)),
        scratch_shapes=[pltpu.VMEM((size, size), F32)] + buffers,
        compiler_params=PARAMS,
    )(far, probe, patch, amplitude[0], power, inverse, forward)
    probe_grad = lax.psum(term, "scan").astype(F32)

    me = lax.axis_index("mode")
    if groups == 2:
        mine = lax.dynamic_index_in_dim(grad, me, 0, keepdims=True)
        other = lax.dynamic_index_in_dim(grad, 1 - me, 0, keepdims=True)
        grad = mine + swap(other)
    else:
        grad = lax.psum(grad, "mode")
    parts = grad.shape[0]
    pieces = pl.pallas_call(
        place_kernel,
        out_shape=jax.ShapeDtypeStruct((devices, parts, rows, size), F32),
        in_specs=[SMEM, SMEM, VMEM],
        out_specs=VMEM,
        scratch_shapes=[pltpu.VMEM((parts, size + 2 * rows + 8, size), F32)],
        compiler_params=PARAMS,
    )(strips, pos_row, grad)
    received = lax.all_to_all(pieces.astype(BF16), "scan", 0, 0, tiled=False).astype(F32)
    strip_grad = pl.pallas_call(
        add_kernel,
        out_shape=jax.ShapeDtypeStruct((parts, rows, cols), F32),
        in_specs=[SMEM, VMEM],
        out_specs=VMEM,
        scratch_shapes=[pltpu.VMEM((parts, rows, padded_cols), F32)],
        compiler_params=PARAMS,
    )(all_cols, received)
    if groups == 2:
        theirs = swap(strip_grad)
        strip_grad = jnp.where(
            me == 0,
            jnp.concatenate([strip_grad, theirs]),
            jnp.concatenate([theirs, strip_grad]),
        )
    return (strip_grad, probe_grad)


def solution(mesh):
    return jax.shard_map(
        shards,
        mesh=mesh,
        in_specs=(
            P(None, "scan", None),
            P("mode", None, None, None),
            P("scan", None, None),
            P("scan"),
            P("scan"),
            P("scan"),
        ),
        out_specs=(P(None, "scan", None), P("mode", None, None, None)),
        check_vma=False,
    )
```

```python
import math

import jax
import jax.numpy as jnp
import numpy as np
from jax import lax
from jax.experimental import pallas as pl
from jax.experimental.pallas import tpu as pltpu
from jax.sharding import PartitionSpec as P

F32 = jnp.float32
BF16 = jnp.bfloat16
LANES = 128
META = 8
PLANE = 4
TILE = 256
PARAMS = pltpu.CompilerParams(vmem_limit_bytes=56 * 1024 * 1024)
VMEM = pl.BlockSpec(memory_space=pltpu.VMEM)
SMEM = pl.BlockSpec(memory_space=pltpu.SMEM)


def dft_tables(size):
    positions = np.arange(size, dtype=np.int32)
    angles = (positions[:, None] * positions[None, :] % size).astype(np.float32)
    angles = angles * np.float32(2.0 * math.pi / size)
    norm = np.float32(1.0 / math.sqrt(size))
    cosine, sine = np.cos(angles) * norm, np.sin(angles) * norm
    forward = np.block([[cosine, sine], [-sine, cosine]])
    inverse = np.block([[cosine, -sine], [sine, cosine]])
    return jnp.asarray(forward, BF16), jnp.asarray(inverse, BF16)


def gather_kernel(mine, out, line_send, line_recv, plane_send, plane_recv, swap_send, swap_recv):
    count = out.shape[1]
    lines = count // PLANE
    scan, mode = lax.axis_index("scan"), lax.axis_index("mode")
    line, place = scan // PLANE, lax.rem(scan, PLANE)
    in_line = [(lax.rem(line + k, lines) * PLANE + place, mode) for k in range(1, lines)]
    in_plane = [(line * PLANE + lax.rem(place + t, PLANE), mode) for t in range(1, PLANE)]
    partner = (scan, 1 - mode)

    barrier = pltpu.get_barrier_semaphore()
    for peer in in_line + in_plane + [partner]:
        pl.semaphore_signal(barrier, inc=1, device_id=peer, device_id_type=pl.DeviceIdType.MESH)
    pl.semaphore_wait(barrier, len(in_line) + len(in_plane) + 1)

    def push(src, dst, send, recv, peer):
        copy = pltpu.make_async_remote_copy(
            src_ref=src,
            dst_ref=dst,
            send_sem=send,
            recv_sem=recv,
            device_id=peer,
            device_id_type=pl.DeviceIdType.MESH,
        )
        copy.start()
        return copy

    own = out.at[mode, scan]
    line_copies = [
        push(mine, own, line_send.at[k], line_recv.at[k], peer) for k, peer in enumerate(in_line)
    ]
    plane_copies = [
        push(mine, own, plane_send.at[0, t], plane_recv.at[0, t], peer) for t, peer in enumerate(in_plane)
    ]
    out[mode, scan] = mine[...]
    for k, arriving in enumerate(line_copies):
        arriving.wait_recv()
        piece = out.at[mode, lax.rem(line + lines - k - 1, lines) * PLANE + place]
        plane_copies += [
            push(piece, piece, plane_send.at[k + 1, t], plane_recv.at[k + 1, t], peer)
            for t, peer in enumerate(in_plane)
        ]
    for copy in plane_copies:
        copy.wait_recv()
    last = push(out.at[mode], out.at[mode], swap_send, swap_recv, partner)
    for copy in line_copies + plane_copies:
        copy.wait_send()
    last.wait()


def cut_kernel(strips, row, col, held, patch, window):
    count, rows = held.shape[1], held.shape[2] - META
    size, cols = patch.shape[-1], held.shape[-1]
    wide = size + LANES

    def place(j, carry):
        at = pl.ds(pl.multiple_of(strips[j] * rows, 8), rows)
        for c in range(2):
            window[c, at, :cols] = held[c, j].astype(F32)[:rows]
        return carry

    lax.fori_loop(0, count, place, 0)
    across = pl.ds(pl.multiple_of(col[0] // LANES * LANES, LANES), wide)
    back = lax.rem(wide - lax.rem(col[0], LANES), wide)
    up = lax.rem(72 - lax.rem(row[0], 8), 72)
    for c in range(2):

        def cut(i, carry, c=c):
            block = window[c, pl.ds(pl.multiple_of(row[0] // 8 * 8 + i * 64, 8), 72), across]
            block = pltpu.roll(block, up, 0)[:64]
            patch[c, pl.ds(pl.multiple_of(i * 64, 64), 64), :] = pltpu.roll(block, back, 1)[:, :size]
            return carry

        lax.fori_loop(0, size // 64, cut, 0)


def forward_kernel(probe, patch, left, right, far, power, wave, half):
    size = patch.shape[-1]

    def leave(i, carry):
        at = pl.ds(pl.multiple_of(i * 64, 64), 64)
        low = pl.ds(pl.multiple_of(size + i * 64, 64), 64)
        pr, pi, xr, xi = probe[0, 0, at], probe[0, 1, at], patch[0, at], patch[1, at]
        wave[at] = (pr * xr - pi * xi).astype(BF16)
        wave[low] = (pr * xi + pi * xr).astype(BF16)
        return carry

    lax.fori_loop(0, size // 64, leave, 0)
    rows_product(left, wave, half)
    first = pl.program_id(0) == 0

    def across(i, carry):
        at = pl.ds(pl.multiple_of(i * TILE, TILE), TILE)
        both = jnp.dot(half[at], right[...], preferred_element_type=F32)
        re, im = both[:, :size], both[:, size:]
        far[0, 0, at] = re
        far[0, 1, at] = im
        here = re * re + im * im
        power[at] = jnp.where(first, here, power[at] + here)
        return carry

    lax.fori_loop(0, size // TILE, across, 0)


def rows_product(left, wave, half):
    size = wave.shape[-1]
    for c in range(2):

        def down(i, carry, c=c):
            at = pl.ds(pl.multiple_of(c * size + i * TILE, TILE), TILE)
            to = pl.ds(pl.multiple_of(i * TILE, TILE), TILE)
            product = jnp.dot(left[at], wave[...], preferred_element_type=F32)
            half[to, c * size : (c + 1) * size] = product.astype(BF16)
            return carry

        lax.fori_loop(0, size // TILE, down, 0)


def backward_kernel(far, probe, patch, measured, power, left, right, term, grad, scale, wave, half):
    size = patch.shape[-1]
    first = pl.program_id(0) == 0

    @pl.when(first)
    def _():
        total = jnp.maximum(power[...], 0.25)
        scale[...] = 1.0 - measured[...] / jnp.sqrt(total)

    def residual(i, carry):
        at = pl.ds(pl.multiple_of(i * 64, 64), 64)
        low = pl.ds(pl.multiple_of(size + i * 64, 64), 64)
        wave[at] = (far[0, 0, at] * scale[at]).astype(BF16)
        wave[low] = (far[0, 1, at] * scale[at]).astype(BF16)
        return carry

    lax.fori_loop(0, size // 64, residual, 0)
    rows_product(left, wave, half)

    def across(i, carry):
        at = pl.ds(pl.multiple_of(i * TILE, TILE), TILE)
        both = jnp.dot(half[at], right[...], preferred_element_type=F32)
        br, bi = both[:, :size], both[:, size:]
        pr, pi, xr, xi = probe[0, 0, at], probe[0, 1, at], patch[0, at], patch[1, at]
        term[0, 0, at] = (xr * br + xi * bi).astype(BF16)
        term[0, 1, at] = (xr * bi - xi * br).astype(BF16)
        re, im = pr * br + pi * bi, pr * bi - pi * br
        grad[0, at] = jnp.where(first, re, grad[0, at] + re)
        grad[1, at] = jnp.where(first, im, grad[1, at] + im)
        return carry

    lax.fori_loop(0, size // TILE, across, 0)


def place_kernel(strips, row, grad, out, padded):
    count, parts, rows, size = out.shape
    padded[...] = jnp.zeros_like(padded)
    padded[:, rows : rows + size, :] = grad[...]

    def one(j, carry):
        start = jnp.clip(strips[j] * rows - row[0], -rows, size) + rows
        base = pl.ds(pl.multiple_of(start // 8 * 8, 8), rows + 8)
        up = lax.rem(rows + 8 - lax.rem(start, 8), rows + 8)
        for k in range(parts):
            out[j, k] = pltpu.roll(padded[k, base, :], up, 0)[:rows]
        return carry

    lax.fori_loop(0, count, one, 0)


def add_kernel(cols, received, out, total):
    count, parts, rows, size = received.shape
    total[...] = jnp.zeros_like(total)
    edge = jnp.zeros((rows, LANES), F32)

    def one(j, carry):
        across = pl.ds(pl.multiple_of(cols[j] // LANES * LANES, LANES), size + LANES)
        shift = lax.rem(cols[j], LANES)
        for k in range(parts):
            piece = jnp.concatenate([received[j, k], edge], axis=1)
            total[k, :, across] += pltpu.roll(piece, shift, 1)
        return carry

    lax.fori_loop(0, count, one, 0)
    out[...] = total[:, :, : out.shape[-1]]


def shards(object_field, probe, amplitude, pos_row, pos_col, strip_of):
    size = probe.shape[-1]
    modes = probe.shape[0]
    rows, cols = object_field.shape[1], object_field.shape[2]
    devices, groups = lax.axis_size("scan"), lax.axis_size("mode")
    padded_cols = cols + LANES
    forward, inverse = dft_tables(size)

    def swap(x):
        return lax.ppermute(x, "mode", [(0, 1), (1, 0)])

    lane = lax.broadcasted_iota(jnp.int32, (2, META, cols), 2)
    numbers = jnp.where(lane == 0, strip_of[0], jnp.where(lane == 1, pos_col[0] // LANES, pos_col[0] % LANES))
    packed = jnp.concatenate([object_field.astype(BF16), numbers.astype(BF16)], axis=1)
    me = lax.axis_index("mode")
    if groups == 2 and devices % PLANE == 0:
        dma, lines = pltpu.SemaphoreType.DMA, devices // PLANE
        held = pl.pallas_call(
            gather_kernel,
            out_shape=jax.ShapeDtypeStruct((2, devices, rows + META, cols), BF16),
            in_specs=[VMEM],
            out_specs=VMEM,
            scratch_shapes=[
                dma((max(lines - 1, 1),)),
                dma((max(lines - 1, 1),)),
                dma((lines, PLANE - 1)),
                dma((lines, PLANE - 1)),
                dma,
                dma,
            ],
            compiler_params=pltpu.CompilerParams(
                vmem_limit_bytes=56 * 1024 * 1024, collective_id=0, has_side_effects=True
            ),
        )(lax.dynamic_index_in_dim(packed, me, 0, keepdims=False))
    else:
        held = lax.all_gather(packed, "scan", axis=1)
    numbers = held[0, :, rows, :3].astype(jnp.int32)
    strips = numbers[:, 0]
    all_cols = numbers[:, 1] * LANES + numbers[:, 2]

    wave_shape = jax.ShapeDtypeStruct((2, size, size), F32)
    patch = pl.pallas_call(
        cut_kernel,
        out_shape=wave_shape,
        in_specs=[SMEM, SMEM, SMEM, VMEM],
        out_specs=VMEM,
        scratch_shapes=[pltpu.VMEM((2, devices * rows + 8, padded_cols), F32)],
        compiler_params=PARAMS,
    )(strips, pos_row, pos_col, held)

    def whole(*shape):
        return pl.BlockSpec(shape, lambda m: (0,) * len(shape))

    mode_spec = pl.BlockSpec((1, 2, size, size), lambda m: (m, 0, 0, 0))
    table_spec = whole(2 * size, 2 * size)
    buffers = [pltpu.VMEM((2 * size, size), BF16), pltpu.VMEM((size, 2 * size), BF16)]
    far, power = pl.pallas_call(
        forward_kernel,
        grid=(modes,),
        out_shape=(
            jax.ShapeDtypeStruct((modes, 2, size, size), F32),
            jax.ShapeDtypeStruct((size, size), F32),
        ),
        in_specs=[mode_spec, whole(2, size, size), table_spec, table_spec],
        out_specs=(mode_spec, whole(size, size)),
        scratch_shapes=buffers,
        compiler_params=PARAMS,
    )(probe, patch, forward, inverse)
    power = power + swap(power) if groups == 2 else lax.psum(power, "mode")
    term, grad = pl.pallas_call(
        backward_kernel,
        grid=(modes,),
        out_shape=(jax.ShapeDtypeStruct((modes, 2, size, size), BF16), wave_shape),
        in_specs=[
            mode_spec,
            mode_spec,
            whole(2, size, size),
            whole(size, size),
            whole(size, size),
            table_spec,
            table_spec,
        ],
        out_specs=(mode_spec, whole(2, size, size)),
        scratch_shapes=[pltpu.VMEM((size, size), F32)] + buffers,
        compiler_params=PARAMS,
    )(far, probe, patch, amplitude[0], power, inverse, forward)
    probe_grad = lax.psum(term, "scan").astype(F32)

    if groups == 2:
        mine = lax.dynamic_index_in_dim(grad, me, 0, keepdims=True)
        other = lax.dynamic_index_in_dim(grad, 1 - me, 0, keepdims=True)
        grad = mine + swap(other)
    else:
        grad = lax.psum(grad, "mode")
    parts = grad.shape[0]
    pieces = pl.pallas_call(
        place_kernel,
        out_shape=jax.ShapeDtypeStruct((devices, parts, rows, size), F32),
        in_specs=[SMEM, SMEM, VMEM],
        out_specs=VMEM,
        scratch_shapes=[pltpu.VMEM((parts, size + 2 * rows + 8, size), F32)],
        compiler_params=PARAMS,
    )(strips, pos_row, grad)
    received = lax.all_to_all(pieces.astype(BF16), "scan", 0, 0, tiled=False).astype(F32)
    strip_grad = pl.pallas_call(
        add_kernel,
        out_shape=jax.ShapeDtypeStruct((parts, rows, cols), F32),
        in_specs=[SMEM, VMEM],
        out_specs=VMEM,
        scratch_shapes=[pltpu.VMEM((parts, rows, padded_cols), F32)],
        compiler_params=PARAMS,
    )(all_cols, received)
    if groups == 2:
        theirs = swap(strip_grad)
        strip_grad = jnp.where(
            me == 0,
            jnp.concatenate([strip_grad, theirs]),
            jnp.concatenate([theirs, strip_grad]),
        )
    return (strip_grad, probe_grad)


def solution(mesh):
    return jax.shard_map(
        shards,
        mesh=mesh,
        in_specs=(
            P(None, "scan", None),
            P("mode", None, None, None),
            P("scan", None, None),
            P("scan"),
            P("scan"),
            P("scan"),
        ),
        out_specs=(P(None, "scan", None), P("mode", None, None, None)),
        check_vma=False,
    )
```

```python
import math

import jax
import jax.numpy as jnp
import numpy as np
from jax import lax
from jax.experimental import pallas as pl
from jax.experimental.pallas import tpu as pltpu
from jax.sharding import PartitionSpec as P

F32 = jnp.float32
BF16 = jnp.bfloat16
LANES = 128
META = 8
PLANE = 4
TILE = 256
PARAMS = pltpu.CompilerParams(vmem_limit_bytes=56 * 1024 * 1024)
VMEM = pl.BlockSpec(memory_space=pltpu.VMEM)
SMEM = pl.BlockSpec(memory_space=pltpu.SMEM)


def dft_tables(size):
    positions = np.arange(size, dtype=np.int32)
    angles = (positions[:, None] * positions[None, :] % size).astype(np.float32)
    angles = angles * np.float32(2.0 * math.pi / size)
    norm = np.float32(1.0 / math.sqrt(size))
    cosine, sine = np.cos(angles) * norm, np.sin(angles) * norm
    forward = np.block([[cosine, sine], [-sine, cosine]])
    inverse = np.block([[cosine, -sine], [sine, cosine]])
    return jnp.asarray(forward, BF16), jnp.asarray(inverse, BF16)


def gather_kernel(mine, out, line_send, line_recv, plane_send, plane_recv, swap_send, swap_recv):
    count = out.shape[1]
    lines = count // PLANE
    scan, mode = lax.axis_index("scan"), lax.axis_index("mode")
    line, place = scan // PLANE, lax.rem(scan, PLANE)
    in_line = [(lax.rem(line + k, lines) * PLANE + place, mode) for k in range(1, lines)]
    in_plane = [(line * PLANE + lax.rem(place + t, PLANE), mode) for t in range(1, PLANE)]
    partner = (scan, 1 - mode)

    barrier = pltpu.get_barrier_semaphore()
    for peer in in_line + in_plane + [partner]:
        pl.semaphore_signal(barrier, inc=1, device_id=peer, device_id_type=pl.DeviceIdType.MESH)
    pl.semaphore_wait(barrier, len(in_line) + len(in_plane) + 1)

    def push(src, dst, send, recv, peer):
        copy = pltpu.make_async_remote_copy(
            src_ref=src,
            dst_ref=dst,
            send_sem=send,
            recv_sem=recv,
            device_id=peer,
            device_id_type=pl.DeviceIdType.MESH,
        )
        copy.start()
        return copy

    own = out.at[mode, scan]
    line_copies = [
        push(mine, own, line_send.at[k], line_recv.at[k], peer) for k, peer in enumerate(in_line)
    ]
    plane_copies = [
        push(mine, own, plane_send.at[0, t], plane_recv.at[0, t], peer) for t, peer in enumerate(in_plane)
    ]
    out[mode, scan] = mine[...]
    for k, arriving in enumerate(line_copies):
        arriving.wait_recv()
        piece = out.at[mode, lax.rem(line + lines - k - 1, lines) * PLANE + place]
        plane_copies += [
            push(piece, piece, plane_send.at[k + 1, t], plane_recv.at[k + 1, t], peer)
            for t, peer in enumerate(in_plane)
        ]
    for copy in plane_copies:
        copy.wait_recv()
    last = push(out.at[mode], out.at[mode], swap_send, swap_recv, partner)
    for copy in line_copies + plane_copies:
        copy.wait_send()
    last.wait()


def cut_kernel(strips, row, col, held, patch, window):
    count, rows = held.shape[1], held.shape[2] - META
    size, cols = patch.shape[-1], held.shape[-1]
    wide = size + LANES

    def place(j, carry):
        at = pl.ds(pl.multiple_of(strips[j] * rows, 8), rows)
        for c in range(2):
            window[c, at, :cols] = held[c, j].astype(F32)[:rows]
        return carry

    lax.fori_loop(0, count, place, 0)
    across = pl.ds(pl.multiple_of(col[0] // LANES * LANES, LANES), wide)
    back = lax.rem(wide - lax.rem(col[0], LANES), wide)
    up = lax.rem(72 - lax.rem(row[0], 8), 72)
    for c in range(2):

        def cut(i, carry, c=c):
            block = window[c, pl.ds(pl.multiple_of(row[0] // 8 * 8 + i * 64, 8), 72), across]
            block = pltpu.roll(block, up, 0)[:64]
            patch[c, pl.ds(pl.multiple_of(i * 64, 64), 64), :] = pltpu.roll(block, back, 1)[:, :size]
            return carry

        lax.fori_loop(0, size // 64, cut, 0)


def forward_kernel(probe, patch, left, right, far, power, wave, half):
    size = patch.shape[-1]

    def leave(i, carry):
        at = pl.ds(pl.multiple_of(i * 64, 64), 64)
        low = pl.ds(pl.multiple_of(size + i * 64, 64), 64)
        pr, pi, xr, xi = probe[0, 0, at], probe[0, 1, at], patch[0, at], patch[1, at]
        wave[at] = (pr * xr - pi * xi).astype(BF16)
        wave[low] = (pr * xi + pi * xr).astype(BF16)
        return carry

    lax.fori_loop(0, size // 64, leave, 0)
    rows_product(left, wave, half)
    first = pl.program_id(0) == 0

    def across(i, carry):
        at = pl.ds(pl.multiple_of(i * TILE, TILE), TILE)
        both = jnp.dot(half[at], right[...], preferred_element_type=F32)
        re, im = both[:, :size], both[:, size:]
        far[0, 0, at] = re
        far[0, 1, at] = im
        here = re * re + im * im
        power[at] = jnp.where(first, here, power[at] + here)
        return carry

    lax.fori_loop(0, size // TILE, across, 0)


def rows_product(left, wave, half):
    size = wave.shape[-1]
    for c in range(2):

        def down(i, carry, c=c):
            at = pl.ds(pl.multiple_of(c * size + i * TILE, TILE), TILE)
            to = pl.ds(pl.multiple_of(i * TILE, TILE), TILE)
            product = jnp.dot(left[at], wave[...], preferred_element_type=F32)
            half[to, c * size : (c + 1) * size] = product.astype(BF16)
            return carry

        lax.fori_loop(0, size // TILE, down, 0)


def backward_kernel(far, probe, patch, measured, power, left, right, term, grad, scale, wave, half):
    size = patch.shape[-1]
    first = pl.program_id(0) == 0

    @pl.when(first)
    def _():
        total = jnp.maximum(power[...], 0.25)
        scale[...] = 1.0 - measured[...] / jnp.sqrt(total)

    def residual(i, carry):
        at = pl.ds(pl.multiple_of(i * 64, 64), 64)
        low = pl.ds(pl.multiple_of(size + i * 64, 64), 64)
        wave[at] = (far[0, 0, at] * scale[at]).astype(BF16)
        wave[low] = (far[0, 1, at] * scale[at]).astype(BF16)
        return carry

    lax.fori_loop(0, size // 64, residual, 0)
    rows_product(left, wave, half)

    def across(i, carry):
        at = pl.ds(pl.multiple_of(i * TILE, TILE), TILE)
        both = jnp.dot(half[at], right[...], preferred_element_type=F32)
        br, bi = both[:, :size], both[:, size:]
        pr, pi, xr, xi = probe[0, 0, at], probe[0, 1, at], patch[0, at], patch[1, at]
        term[0, 0, at] = (xr * br + xi * bi).astype(BF16)
        term[0, 1, at] = (xr * bi - xi * br).astype(BF16)
        re, im = pr * br + pi * bi, pr * bi - pi * br
        grad[0, at] = jnp.where(first, re, grad[0, at] + re)
        grad[1, at] = jnp.where(first, im, grad[1, at] + im)
        return carry

    lax.fori_loop(0, size // TILE, across, 0)


def place_kernel(strips, row, grad, out, padded):
    count, parts, rows, size = out.shape
    padded[...] = jnp.zeros_like(padded)
    padded[:, rows : rows + size, :] = grad[...]

    def one(j, carry):
        start = jnp.clip(strips[j] * rows - row[0], -rows, size) + rows
        base = pl.ds(pl.multiple_of(start // 8 * 8, 8), rows + 8)
        up = lax.rem(rows + 8 - lax.rem(start, 8), rows + 8)
        for k in range(parts):
            out[j, k] = pltpu.roll(padded[k, base, :], up, 0)[:rows]
        return carry

    lax.fori_loop(0, count, one, 0)


def add_kernel(cols, received, out, total):
    count, parts, rows, size = received.shape
    total[...] = jnp.zeros_like(total)
    edge = jnp.zeros((rows, LANES), F32)

    def one(j, carry):
        across = pl.ds(pl.multiple_of(cols[j] // LANES * LANES, LANES), size + LANES)
        shift = lax.rem(cols[j], LANES)
        for k in range(parts):
            piece = jnp.concatenate([received[j, k], edge], axis=1)
            total[k, :, across] += pltpu.roll(piece, shift, 1)
        return carry

    lax.fori_loop(0, count, one, 0)
    out[...] = total[:, :, : out.shape[-1]]


def shards(object_field, probe, amplitude, pos_row, pos_col, strip_of):
    size = probe.shape[-1]
    modes = probe.shape[0]
    rows, cols = object_field.shape[1], object_field.shape[2]
    devices, groups = lax.axis_size("scan"), lax.axis_size("mode")
    padded_cols = cols + LANES
    forward, inverse = dft_tables(size)

    def swap(x):
        return lax.ppermute(x, "mode", [(0, 1), (1, 0)])

    lane = lax.broadcasted_iota(jnp.int32, (2, META, cols), 2)
    numbers = jnp.where(lane == 0, strip_of[0], jnp.where(lane == 1, pos_col[0] // LANES, pos_col[0] % LANES))
    packed = jnp.concatenate([object_field.astype(BF16), numbers.astype(BF16)], axis=1)
    me = lax.axis_index("mode")
    if groups == 2 and devices % PLANE == 0:
        dma, lines = pltpu.SemaphoreType.DMA, devices // PLANE
        held = pl.pallas_call(
            gather_kernel,
            out_shape=jax.ShapeDtypeStruct((2, devices, rows + META, cols), BF16),
            in_specs=[VMEM],
            out_specs=VMEM,
            scratch_shapes=[
                dma((max(lines - 1, 1),)),
                dma((max(lines - 1, 1),)),
                dma((lines, PLANE - 1)),
                dma((lines, PLANE - 1)),
                dma,
                dma,
            ],
            compiler_params=pltpu.CompilerParams(
                vmem_limit_bytes=56 * 1024 * 1024, collective_id=0, has_side_effects=True
            ),
        )(lax.dynamic_index_in_dim(packed, me, 0, keepdims=False))
    else:
        held = lax.all_gather(packed, "scan", axis=1)
    numbers = held[0, :, rows, :3].astype(jnp.int32)
    strips = numbers[:, 0]
    all_cols = numbers[:, 1] * LANES + numbers[:, 2]

    wave_shape = jax.ShapeDtypeStruct((2, size, size), F32)
    patch = pl.pallas_call(
        cut_kernel,
        out_shape=wave_shape,
        in_specs=[SMEM, SMEM, SMEM, VMEM],
        out_specs=VMEM,
        scratch_shapes=[pltpu.VMEM((2, devices * rows + 8, padded_cols), F32)],
        compiler_params=PARAMS,
    )(strips, pos_row, pos_col, held)

    def whole(*shape):
        return pl.BlockSpec(shape, lambda m: (0,) * len(shape))

    mode_spec = pl.BlockSpec((1, 2, size, size), lambda m: (m, 0, 0, 0))
    table_spec = whole(2 * size, 2 * size)
    buffers = [pltpu.VMEM((2 * size, size), BF16), pltpu.VMEM((size, 2 * size), BF16)]
    far, power = pl.pallas_call(
        forward_kernel,
        grid=(modes,),
        out_shape=(
            jax.ShapeDtypeStruct((modes, 2, size, size), F32),
            jax.ShapeDtypeStruct((size, size), F32),
        ),
        in_specs=[mode_spec, whole(2, size, size), table_spec, table_spec],
        out_specs=(mode_spec, whole(size, size)),
        scratch_shapes=buffers,
        compiler_params=PARAMS,
    )(probe, patch, forward, inverse)
    power = power + swap(power) if groups == 2 else lax.psum(power, "mode")
    cuts = [0, modes // 2, modes] if modes > 1 else [0, modes]
    probe_parts, grad = [], 0.0
    for low, high in zip(cuts[:-1], cuts[1:]):
        from_spec = pl.BlockSpec((1, 2, size, size), lambda m, low=low: (m + low, 0, 0, 0))
        term, grad_part = pl.pallas_call(
            backward_kernel,
            grid=(high - low,),
            out_shape=(jax.ShapeDtypeStruct((high - low, 2, size, size), BF16), wave_shape),
            in_specs=[
                from_spec,
                from_spec,
                whole(2, size, size),
                whole(size, size),
                whole(size, size),
                table_spec,
                table_spec,
            ],
            out_specs=(mode_spec, whole(2, size, size)),
            scratch_shapes=[pltpu.VMEM((size, size), F32)] + buffers,
            compiler_params=PARAMS,
        )(far, probe, patch, amplitude[0], power, inverse, forward)
        probe_parts.append(lax.psum(term, "scan"))
        grad = grad + grad_part
    probe_grad = jnp.concatenate(probe_parts).astype(F32)

    if groups == 2:
        mine = lax.dynamic_index_in_dim(grad, me, 0, keepdims=True)
        other = lax.dynamic_index_in_dim(grad, 1 - me, 0, keepdims=True)
        grad = mine + swap(other)
    else:
        grad = lax.psum(grad, "mode")
    parts = grad.shape[0]
    pieces = pl.pallas_call(
        place_kernel,
        out_shape=jax.ShapeDtypeStruct((devices, parts, rows, size), F32),
        in_specs=[SMEM, SMEM, VMEM],
        out_specs=VMEM,
        scratch_shapes=[pltpu.VMEM((parts, size + 2 * rows + 8, size), F32)],
        compiler_params=PARAMS,
    )(strips, pos_row, grad)
    received = lax.all_to_all(pieces.astype(BF16), "scan", 0, 0, tiled=False).astype(F32)
    strip_grad = pl.pallas_call(
        add_kernel,
        out_shape=jax.ShapeDtypeStruct((parts, rows, cols), F32),
        in_specs=[SMEM, VMEM],
        out_specs=VMEM,
        scratch_shapes=[pltpu.VMEM((parts, rows, padded_cols), F32)],
        compiler_params=PARAMS,
    )(all_cols, received)
    if groups == 2:
        theirs = swap(strip_grad)
        strip_grad = jnp.where(
            me == 0,
            jnp.concatenate([strip_grad, theirs]),
            jnp.concatenate([theirs, strip_grad]),
        )
    return (strip_grad, probe_grad)


def solution(mesh):
    return jax.shard_map(
        shards,
        mesh=mesh,
        in_specs=(
            P(None, "scan", None),
            P("mode", None, None, None),
            P("scan", None, None),
            P("scan"),
            P("scan"),
            P("scan"),
        ),
        out_specs=(P(None, "scan", None), P("mode", None, None, None)),
        check_vma=False,
    )
```
